128 devices in a mesh: section: 64 (over z, y, x_hi, core), cfg: 2 (over x_lo).
Axes of the slice: x: 4 (x_hi: 2, x_lo: 2; x = x_hi * 2 + x_lo), y: 4, z: 4, core: 2. Of those that a mesh axis runs over, the one named last changes fastest.
Arguments:
- patches: bfloat16 [64, 384, 3072], P('section', 'cfg'), may hold values from -6 to 6
- patch_index: int32 [64], replicated, may hold values from 0 to 3
- step_index: int32 [64], replicated, may hold values from 0 to 27
- counts: int32 [4], replicated, may hold values from 1 to 384, 1152 in all
- modulation: bfloat16 [64, 28, 3, 3072], P('section'), may hold values from -3 to 3
- qk_gain: float32 [64, 2, 128], P('section'), may hold values from 0.6 to 4.5
- w_qkv: bfloat16 [64, 3, 3072, 1536], P('section', None, None, 'cfg'), may hold values from -0.108253175 to 0.108253175
- w_out: bfloat16 [64, 1536, 3072], P('section', 'cfg'), may hold values from -0.15625 to 0.15625
- cache_k: bfloat16 [64, 1792, 1536], P('section', None, 'cfg'), may hold values from -6 to 6
- cache_v: bfloat16 [64, 1792, 1536], P('section', None, 'cfg'), may hold values from -6 to 6
Outputs:
- result: bfloat16 [64, 384, 3072], P('section', 'cfg')
The draws below stay inside these ranges and needn't reach their ends.
Inputs may be any that keep to these rules, and one draw needn't show every extreme that they name: `counts`: some patch is full.
All inputs are finite; a program needn't handle non-finite values.
Results may differ from the reference program's by a relative error of at most 0.015.
Values may be sent and summed in bfloat16 or wider, within the bound.
No kernel may reach another device: no remote copies, remote signals or barrier semaphores. Data moves between devices by JAX's collectives and lax.ppermute only.
A program may use at most 192 MiB of HBM per device.

```python
import math
import jax
import jax.numpy as jnp
import numpy as np
from jax import lax

D = 3072
HD = 128
HEADS = 12
PATCH_TOK = 384
NPATCH = 4
TEXT = 256
STEPS = 28
TICKS = 2
SEQ = 1792
N_SECTION = 64


def draw_modulation(key, part):
    own_key = jax.random.fold_in(key, 11)
    key_base = jax.random.fold_in(own_key, 0)
    drawn = jnp.clip(0.5 * jax.random.normal(key_base, (N_SECTION, STEPS, 3, D), jnp.float32), -3.0, 3.0)
    return drawn.astype(jnp.bfloat16)


def draw_qk_gain(key, part):
    own_key = jax.random.fold_in(key, 7)
    level = jax.random.uniform(own_key, (N_SECTION, 2, HD), jnp.float32)
    low, high = (math.log(0.6), math.log(2.0))
    gains = jnp.exp(low + (high - low) * level)
    return gains


def draw_w_qkv(key, part):
    own_key = jax.random.fold_in(key, 23)
    key_query, key_keys, key_values = jax.random.split(own_key, 3)
    shape = (N_SECTION, D, HEADS * HD)
    factor = D ** (-0.5)
    w_query = jnp.clip(jax.random.normal(key_query, shape, jnp.float32), -6.0, 6.0) * factor
    w_keys = jnp.clip(jax.random.normal(key_keys, shape, jnp.float32), -6.0, 6.0) * factor
    w_values = jnp.clip(jax.random.normal(key_values, shape, jnp.float32), -6.0, 6.0) * factor
    return jnp.stack([w_query, w_keys, w_values], axis=1).astype(jnp.bfloat16)


def plant(values, key, low, top_value):
    longest = values.shape.index(max(values.shape))
    spots = []
    for shift in (0, 1):
        where = [jax.random.randint(jax.random.fold_in(key, axis), (), 0, length) for axis, length in enumerate(values.shape)]
        where[longest] = (where[longest] + shift) % values.shape[longest]
        spots.append(tuple(where))
    return values.at[spots[0]].set(low).at[spots[1]].set(top_value)


def levels(key, extent, shards, least, high):
    def one(dim, parts):
        draws = jax.random.uniform(jax.random.fold_in(jax.random.fold_in(key, 6), dim), (parts,), jnp.float32, least / len(shards), high / len(shards))
        return jnp.repeat(jnp.exp(draws), extent[dim] // parts).reshape((-1,) + (1,) * (len(extent) - dim - 1))

    level = one(*shards[0])
    for cut in shards[1:]:
        level = level * one(*cut)
    return level


def split_up(count, total, bound, lean):
    weights = [(1 << 20) // math.isqrt(standing ** lean) + 1 for standing in range(2, count + 1)]
    spare, given = total - bound - (count - 1), [1] * (count - 1)
    while spare > 0:
        free = [i for i in range(count - 1) if given[i] < bound]
        pool, left = sum([weights[i] for i in free]), spare
        for i in free:
            addition = min(bound - given[i], max(1, left * weights[i] // pool), spare)
            given[i] = given[i] + addition
            spare = spare - addition
    return np.array([bound] + given)


def ragged(key, count, total, reach, slope):
    if count == 2:
        one = jax.random.randint(key, (), max(1, total - reach), min(reach, total - 1) + 1)
        return jnp.stack([one, total - one])
    tallies = jnp.asarray(split_up(count, total, reach, slope), jnp.int32)
    pairs = (count - 1) // 2
    giver, sink = tallies[1:1 + 2 * pairs:2], tallies[2:2 + 2 * pairs:2]
    slack = jnp.minimum(giver - 1, reach - sink)
    shifted = jax.random.randint(jax.random.fold_in(key, 1), (pairs,), 0, 1 << 20) % (slack + 1)
    tallies = tallies.at[1:1 + 2 * pairs:2].set(giver - shifted).at[2:2 + 2 * pairs:2].set(sink + shifted)
    return tallies[jax.random.permutation(jax.random.fold_in(key, 2), count)]


def noise(key, shape, scale, limit, pieces=(), kind=jnp.bfloat16):
    values = jax.random.normal(key, shape, jnp.float32) * scale
    if len(pieces) > 0:
        values = levels(key, shape, pieces, -0.22, 0.18) * values
    return jnp.clip(values, min=-limit, max=limit).astype(kind)


def setup_inputs(seed: int = 0) -> dict:
    arg_keys = jax.random.split(jax.random.key(seed), 11)
    patches = noise(arg_keys[0], (N_SECTION, PATCH_TOK, D), 1.0, 6.0, ((0, 64), (1, 2)))
    patch_index = plant(jax.random.randint(arg_keys[1], (N_SECTION,), 0, NPATCH), jax.random.fold_in(arg_keys[1], 1), 0, NPATCH - 1).astype(jnp.int32)
    step_index = plant(jax.random.randint(arg_keys[2], (N_SECTION,), 0, STEPS), jax.random.fold_in(arg_keys[2], 1), 0, STEPS - 1).astype(jnp.int32)
    counts = ragged(arg_keys[3], NPATCH, NPATCH * PATCH_TOK * 3 // 4, PATCH_TOK, 1).astype(jnp.int32)
    modulation = draw_modulation(jax.random.fold_in(arg_keys[10], 71), 0)
    qk_gain = draw_qk_gain(jax.random.fold_in(arg_keys[10], 71), 0)
    w_qkv = draw_w_qkv(jax.random.fold_in(arg_keys[10], 71), 0)
    w_out = noise(arg_keys[7], (N_SECTION, HEADS * HD, D), (HEADS * HD) ** -0.5, 0.15625, ((0, 64), (1, 2)))
    cache_k = noise(arg_keys[8], (N_SECTION, SEQ, HEADS * HD), 1.0, 6.0, ((0, 64), (2, 2)))
    cache_v = noise(arg_keys[9], (N_SECTION, SEQ, HEADS * HD), 1.0, 6.0, ((0, 64), (2, 2)))
    return dict(patches=patches, patch_index=patch_index, step_index=step_index, counts=counts, modulation=modulation, qk_gain=qk_gain, w_qkv=w_qkv, w_out=w_out, cache_k=cache_k, cache_v=cache_v)


def valid_keys(counts):
    places = jnp.arange(SEQ, dtype=jnp.int32)
    inside = places - TEXT
    which = jnp.clip(inside // PATCH_TOK, 0, NPATCH - 1).astype(jnp.int32)
    offset = inside - which * PATCH_TOK
    return (places < TEXT) | (offset < counts[which])

def head_norm(proj, gain):
    heads = proj.reshape(proj.shape[0], -1, HD)
    scaled = heads * lax.rsqrt(lax.optimization_barrier(jnp.mean(heads * heads, axis=-1, keepdims=True)) + 1e-06) * gain
    return scaled.astype(jnp.bfloat16)

def one_layer(rows, current, mods, gains, w_qkv, w_out, keys, values, valid):
    wide = rows.astype(jnp.float32)
    mean = lax.optimization_barrier(jnp.mean(wide, axis=-1, keepdims=True))
    spread = lax.optimization_barrier(jnp.mean((wide - mean) ** 2, axis=-1, keepdims=True))
    normed = (wide - mean) * lax.rsqrt(spread + 1e-06)
    hidden = (normed * (1.0 + mods[1]) + mods[0]).astype(jnp.bfloat16)
    query = head_norm(jnp.dot(hidden, w_qkv[0], preferred_element_type=jnp.float32), gains[0])
    fresh_k = head_norm(jnp.dot(hidden, w_qkv[1], preferred_element_type=jnp.float32), gains[1])
    fresh_v = jnp.dot(hidden, w_qkv[2], preferred_element_type=jnp.float32).astype(jnp.bfloat16)
    start = (TEXT + current * PATCH_TOK).astype(jnp.int32)
    zero = jnp.zeros((), jnp.int32)
    keys = lax.dynamic_update_slice(keys, fresh_k.reshape(rows.shape[0], -1), (start, zero))
    values = lax.dynamic_update_slice(values, fresh_v, (start, zero))
    key_heads = keys.reshape(SEQ, -1, HD).astype(jnp.float32)
    value_heads = values.reshape(SEQ, -1, HD).astype(jnp.float32)
    scores = jnp.einsum('qhd,khd->hqk', query.astype(jnp.float32), key_heads) * HD ** (-0.5)
    scores = jnp.where(valid[None, None, :], scores, -1e+30)
    peak = lax.optimization_barrier(jnp.max(scores, axis=-1, keepdims=True))
    expo = jnp.exp(scores - peak)
    weights = (expo / lax.optimization_barrier(jnp.sum(expo, axis=-1, keepdims=True))).astype(jnp.bfloat16)
    attended = jnp.einsum('hqk,khd->qhd', weights.astype(jnp.float32), value_heads)
    attended = attended.astype(jnp.bfloat16).reshape(rows.shape[0], -1)
    mixed = jnp.dot(attended, w_out, preferred_element_type=jnp.float32)
    return ((wide + mods[2] * mixed).astype(jnp.bfloat16), keys, values)

def reference(patches, patch_index, step_index, counts, modulation, qk_gain, w_qkv, w_out, cache_k, cache_v):
    valid = valid_keys(counts)
    section_count = patches.shape[0]
    section_rows = jnp.arange(section_count, dtype=jnp.int32)
    acts = patches
    held = patch_index
    held_steps = step_index
    for tick in range(TICKS):
        mods_all = modulation[section_rows, held_steps].astype(jnp.float32)

        def apply(items):
            rows, current, mods, gains, wq, wo, keys, values = items
            return one_layer(rows, current, mods, gains, wq, wo, keys, values, valid)
        outs, cache_k, cache_v = lax.map(apply, (acts, held, mods_all, qk_gain, w_qkv, w_out, cache_k, cache_v))
        acts = jnp.roll(outs, 1, axis=0)
        held = jnp.roll(held, 1, axis=0)
        held_steps = jnp.roll(held_steps, 1, axis=0)
    return acts
```

```python
import jax
import jax.numpy as jnp
from jax import lax
from jax.experimental import pallas as pl
from jax.experimental.pallas import tpu as pltpu
from jax.sharding import PartitionSpec as P

HD = 128
PATCH_TOK = 384
NPATCH = 4
TEXT = 256
TICKS = 2
VMEM = pl.BlockSpec(memory_space=pltpu.VMEM)
SMEM = pl.BlockSpec(memory_space=pltpu.SMEM)
BF16 = jnp.bfloat16
F32 = jnp.float32


def held(array):
    return pltpu.with_memory_space_constraint(array, pltpu.VMEM)


def modulated(rows, mods):
    wide = rows.astype(F32)
    mean = jnp.mean(wide, axis=-1, keepdims=True)
    centred = wide - mean
    spread = jnp.mean(centred * centred, axis=-1, keepdims=True)
    normed = centred * lax.rsqrt(spread + 1e-06)
    return (normed * (1.0 + mods[1:2]) + mods[0:1]).astype(BF16)


def head_norm(proj, gain):
    parts = []
    for head in range(proj.shape[1] // HD):
        x = proj[:, head * HD : (head + 1) * HD]
        scale = lax.rsqrt(jnp.mean(x * x, axis=-1, keepdims=True) + 1e-06)
        parts.append((x * scale * gain).astype(BF16))
    return jnp.concatenate(parts, axis=1)


def qkv_kernel(where, rows, mods, gains, w_qkv, keys_in, values_in, query, keys, values):
    del keys_in, values_in
    hidden = modulated(rows[...], mods[...])
    start = pl.multiple_of(where[0], 64)
    here = pl.ds(start, rows.shape[0])
    keys[here, :] = head_norm(jnp.dot(hidden, w_qkv[1], preferred_element_type=F32), gains[1:2])
    values[here, :] = jnp.dot(hidden, w_qkv[2], preferred_element_type=F32).astype(BF16)
    query[...] = head_norm(jnp.dot(hidden, w_qkv[0], preferred_element_type=F32), gains[0:1])


def qkv(where, rows, mods, gains, w_qkv, keys, values):
    count, width = rows.shape[0], keys.shape[1]
    return pl.pallas_call(
        qkv_kernel,
        in_specs=[SMEM, VMEM, VMEM, VMEM, VMEM, VMEM, VMEM],
        out_specs=[VMEM, VMEM, VMEM],
        out_shape=[
            jax.ShapeDtypeStruct((count, width), BF16),
            pltpu.VMEM(keys.shape, BF16),
            pltpu.VMEM(values.shape, BF16),
        ],
        input_output_aliases={5: 1, 6: 2},
        compiler_params=pltpu.CompilerParams(vmem_limit_bytes=16 * 1024 * 1024),
        cost_estimate=pl.CostEstimate(
            flops=2 * count * rows.shape[1] * 3 * width, bytes_accessed=count * 10000, transcendentals=0
        ),
        name="qkv",
    )(where, rows, mods, gains, w_qkv, held(keys), held(values))


def attended(query, keys, values, counts):
    total = keys.shape[0]
    place = lax.broadcasted_iota(jnp.int32, (1, total), 1)
    valid = place < TEXT
    for patch in range(NPATCH):
        begin = TEXT + patch * PATCH_TOK
        valid |= (place >= begin) & (place < begin + counts[patch])
    bias = jnp.where(valid, 0.0, -1e30)
    outs = []
    for head in range(keys.shape[1] // HD):
        cols = slice(head * HD, (head + 1) * HD)
        scores = lax.dot_general(
            query[:, cols], keys[:, cols], (((1,), (1,)), ((), ())), preferred_element_type=F32
        )
        scores = scores + bias
        peak = jnp.max(scores, axis=-1, keepdims=True)
        expo = jnp.exp((scores - peak) * HD ** (-0.5))
        total_weight = jnp.sum(expo, axis=-1, keepdims=True)
        out = jnp.dot(expo.astype(BF16), values[:, cols], preferred_element_type=F32)
        outs.append((out / total_weight).astype(BF16))
    return jnp.concatenate(outs, axis=1)


def send_kernel(counts, query, keys, values, w_out, part):
    out = attended(query, keys, values, counts)
    part[...] = jnp.dot(out, w_out[...], preferred_element_type=F32).astype(BF16)


def keep_kernel(counts, query, keys, values, w_out, rows, mods, part):
    out = attended(query, keys, values, counts)
    mixed = jnp.dot(out, w_out[...], preferred_element_type=F32)
    part[...] = rows[...].astype(F32) + mods[2:3] * mixed


def attend(counts, query, keys, values, w_out, rows=None, mods=None):
    count, model = query.shape[0], w_out.shape[1]
    extra = () if rows is None else (rows, mods)
    return pl.pallas_call(
        send_kernel if rows is None else keep_kernel,
        in_specs=[SMEM] + [VMEM] * (4 + len(extra)),
        out_specs=VMEM,
        out_shape=jax.ShapeDtypeStruct((count, model), BF16 if rows is None else F32),
        compiler_params=pltpu.CompilerParams(vmem_limit_bytes=16 * 1024 * 1024),
        cost_estimate=pl.CostEstimate(
            flops=2 * count * query.shape[1] * (2 * keys.shape[0] + model), bytes_accessed=count * 10000,
            transcendentals=count * keys.shape[0] * 6,
        ),
        name="attend",
    )(counts, query, held(keys), held(values), w_out, *extra)


def combine_kernel(base, received, mods, out):
    out[...] = (base[...] + mods[2:3] * received[...].astype(F32)).astype(BF16)


def combine(base, received, mods):
    return pl.pallas_call(
        combine_kernel,
        in_specs=[VMEM] * 3,
        out_specs=VMEM,
        out_shape=jax.ShapeDtypeStruct(received.shape, BF16),
        name="combine",
    )(base, received, mods)


CHUNK = 64


def on_device(
    patches, patch_index, step_index, counts, modulation, qk_gain, w_qkv, w_out, cache_k, cache_v
):
    gains = qk_gain[0]
    weights_in = held(w_qkv[0])
    weights_out = held(w_out[0])
    keys = cache_k[0]
    values = cache_v[0]
    section = lax.axis_index("section")
    sections = lax.axis_size("section")
    half = patches.shape[1]
    chunks = half // CHUNK
    swap = [(0, 1), (1, 0)]
    shift = []
    for s in range(sections):
        for c in range(2):
            to = c if s % 2 == 0 else 1 - c
            shift.append((2 * s + c, 2 * ((s + 1) % sections) + to))

    def exchange(block):
        return lax.ppermute(block, "cfg", swap)

    own = [patches[0, i * CHUNK : (i + 1) * CHUNK] for i in range(chunks)]
    group = lax.axis_index("cfg")
    for tick in range(TICKS):
        source = (section - tick) % sections
        first = TEXT + patch_index[source] * PATCH_TOK
        mods = modulation[0, step_index[source]].astype(F32)
        mine = group if tick == 0 else jnp.where(section % 2 == 1, group, 1 - group)
        other = [exchange(block) for block in own]
        rows = (own, other)
        queries = ([], [])
        for side in range(2):
            begin = first + (mine if side == 0 else 1 - mine) * half
            for i in range(chunks):
                spot = (begin + i * CHUNK).reshape(1)
                q, keys, values = qkv(spot, rows[side][i], mods, gains, weights_in, keys, values)
                queries[side].append(q)
        kept = 0 if tick == 0 else 1
        sent = [attend(counts, q, keys, values, weights_out) for q in queries[1 - kept]]
        got = [exchange(block) for block in sent]
        base = [
            attend(counts, q, keys, values, weights_out, rows[kept][i], mods)
            for i, q in enumerate(queries[kept])
        ]
        done = [combine(base[i], got[i], mods) for i in range(chunks)]
        own = [lax.ppermute(block, ("section", "cfg"), shift) for block in done]
    return jnp.concatenate(own, axis=0)[None]


def solution(mesh):
    in_specs = (
        P("section", "cfg", None),
        P(),
        P(),
        P(),
        P("section", None, None, None),
        P("section", None, None),
        P("section", None, None, "cfg"),
        P("section", "cfg", None),
        P("section", None, "cfg"),
        P("section", None, "cfg"),
    )
    out_specs = P("section", "cfg", None)
    return jax.shard_map(
        on_device, mesh=mesh, in_specs=in_specs, out_specs=out_specs, check_vma=False
    )
```

```python
import jax
import jax.numpy as jnp
from jax import lax
from jax.experimental import pallas as pl
from jax.experimental.pallas import tpu as pltpu
from jax.sharding import PartitionSpec as P

HD = 128
PATCH_TOK = 384
NPATCH = 4
TEXT = 256
SECTIONS = 64
BF16 = jnp.bfloat16
F32 = jnp.float32
VMEM = pl.BlockSpec(memory_space=pltpu.VMEM)
SMEM = pl.BlockSpec(memory_space=pltpu.SMEM)
HBM = pl.BlockSpec(memory_space=pltpu.HBM)
MIB = 1024 * 1024
QUERY_SCALE = HD ** (-0.5) * 1.4426950408889634
MID = (96, 96)
LAST = (96, 64, 32)


def held(array):
    return pltpu.with_memory_space_constraint(array, pltpu.VMEM)


def far(array):
    return pltpu.with_memory_space_constraint(array, pltpu.HBM)


def in_vmem(shape, dtype):
    return pltpu.VMEM(shape, dtype)


def loose(shape, dtype):
    return jax.ShapeDtypeStruct(shape, dtype)


def modulated(rows, mods):
    wide = rows.astype(F32)
    mean = jnp.mean(wide, axis=-1, keepdims=True)
    centred = wide - mean
    spread = jnp.mean(centred * centred, axis=-1, keepdims=True)
    normed = centred * lax.rsqrt(spread + 1e-06)
    return (normed * (1.0 + mods[1:2]) + mods[0:1]).astype(BF16)


def head_norm(proj, gain):
    parts = []
    for head in range(proj.shape[1] // HD):
        x = proj[:, head * HD : (head + 1) * HD]
        scale = lax.rsqrt(jnp.mean(x * x, axis=-1, keepdims=True) + 1e-06)
        parts.append((x * scale * gain).astype(BF16))
    return jnp.concatenate(parts, axis=1)


def project(hidden, weights):
    return jnp.dot(hidden, weights, preferred_element_type=F32)


def limit(mib):
    return pltpu.CompilerParams(vmem_limit_bytes=mib * MIB)


def cost(flops):
    return pl.CostEstimate(flops=int(flops), bytes_accessed=1000000, transcendentals=0)


def first_row(tick, side, patch_index, half):
    section, group = lax.axis_index("section"), lax.axis_index("cfg")
    source = lax.rem(section + SECTIONS - tick, SECTIONS)
    swapped = 0 if tick == 0 else 1 - lax.rem(section, 2)
    which = lax.rem(group + swapped + side, 2)
    return pl.multiple_of(TEXT + patch_index[source] * PATCH_TOK + which * half, 32)


def stream(source, near, sems):
    copies = [pltpu.make_async_copy(source.at[i], near.at[i], sems.at[i]) for i in (1, 2, 0)]
    for copy in copies:
        copy.start()
    return copies


def projections(hidden, gains, near, copies, put_key, put_value, query):
    copies[0].wait()
    put_key(head_norm(project(hidden, near[1]), gains[1:2]))
    copies[1].wait()
    put_value(project(hidden, near[2]).astype(BF16))
    copies[2].wait()
    query[...] = head_norm(project(hidden, near[0]), gains[0:1] * QUERY_SCALE)


def selected(modulation, step):
    at = lax.broadcasted_iota(jnp.int32, (modulation.shape[1], 1), 0) == step
    rows = [
        jnp.sum(jnp.where(at, modulation[i].astype(F32), 0.0), axis=0, keepdims=True)
        for i in range(modulation.shape[0])
    ]
    return jnp.concatenate(rows, axis=0)


def open_kernel(
    patch_far, step_far, rows_far, modulation_far, gains_far, w_qkv, w_out_far, keys_far, values_far,
    query, rows, mods_now, mods_next, gains, w_out, keys, values,
    near, modulation, patch_index, step_index, sems, more,
):
    pairs = [
        (patch_far, patch_index),
        (step_far, step_index),
        (gains_far, gains),
        (modulation_far, modulation),
        (rows_far, rows),
        (keys_far, keys),
        (values_far, values),
        (w_out_far, w_out),
    ]
    others = [pltpu.make_async_copy(a, b, more.at[i]) for i, (a, b) in enumerate(pairs)]
    for copy in others[:5]:
        copy.start()
    copies = stream(w_qkv, near, sems)
    for copy in others[5:]:
        copy.start()
    section = lax.axis_index("section")
    for copy in others[:4]:
        copy.wait()
    mods = selected(modulation, step_index[section])
    mods_now[...] = mods
    mods_next[...] = selected(modulation, step_index[lax.rem(section + SECTIONS - 1, SECTIONS)])
    others[4].wait()
    hidden = modulated(rows[...], mods)
    here = pl.ds(first_row(0, 0, patch_index, rows.shape[0]), rows.shape[0])

    def put_key(fresh):
        others[5].wait()
        keys[here, :] = fresh

    def put_value(fresh):
        others[6].wait()
        values[here, :] = fresh

    projections(hidden, gains[...], near, copies, put_key, put_value, query)
    others[7].wait()


def opening(patch_index, step_index, rows, modulation, gains, w_qkv, w_out, keys, values):
    model = rows.shape[1]
    return pl.pallas_call(
        open_kernel,
        in_specs=[HBM] * 9,
        out_specs=[VMEM] * 8,
        out_shape=[
            in_vmem((rows.shape[0], keys.shape[1]), BF16),
            in_vmem(rows.shape, BF16),
            loose((3, model), F32),
            loose((3, model), F32),
            loose(gains.shape, F32),
            in_vmem(w_out.shape, BF16),
            in_vmem(keys.shape, BF16),
            in_vmem(values.shape, BF16),
        ],
        scratch_shapes=[
            pltpu.VMEM(w_qkv.shape, BF16),
            pltpu.VMEM(modulation.shape, BF16),
            pltpu.SMEM(patch_index.shape, jnp.int32),
            pltpu.SMEM(step_index.shape, jnp.int32),
            pltpu.SemaphoreType.DMA((3,)),
            pltpu.SemaphoreType.DMA((8,)),
        ],
        compiler_params=limit(26),
        cost_estimate=cost(2 * w_qkv.size * 256),
        name="opening",
    )(*map(far, (patch_index, step_index, rows, modulation, gains, w_qkv, w_out, keys, values)))


def qkv(tick, side, patch_index, pieces, mods, gains, w_qkv, keys, values, either=False):
    count = pieces[0].shape[0] if either else sum(p.shape[0] for p in pieces)
    half, model, width = count, pieces[0].shape[1], keys.shape[1]
    n = len(pieces)

    def kernel(patch_index, *refs):
        parts, (mods, gains, w_qkv, _, _) = refs[:n], refs[n : n + 5]
        query, keys, values, near, sems = refs[n + 5 :]
        copies = stream(w_qkv, near, sems)
        if either:
            rows = parts[0][...] + parts[1][...]
        else:
            rows = jnp.concatenate([p[...] for p in parts], axis=0)
        hidden = modulated(rows, mods[...])
        here = pl.ds(first_row(tick, side, patch_index, half), count)

        def put_key(fresh):
            keys[here, :] = fresh

        def put_value(fresh):
            values[here, :] = fresh

        projections(hidden, gains[...], near, copies, put_key, put_value, query)

    return pl.pallas_call(
        kernel,
        in_specs=[SMEM] + [VMEM] * (n + 2) + [HBM, VMEM, VMEM],
        out_specs=[VMEM] * 3,
        out_shape=[in_vmem((count, width), BF16), in_vmem(keys.shape, BF16), in_vmem(values.shape, BF16)],
        input_output_aliases={n + 4: 1, n + 5: 2},
        scratch_shapes=[pltpu.VMEM(w_qkv.shape, BF16), pltpu.SemaphoreType.DMA((3,))],
        compiler_params=limit(26),
        cost_estimate=cost(2 * w_qkv.size * 256),
        name="qkv",
    )(patch_index, *pieces, mods, gains, far(w_qkv), held(keys), held(values))


def attended(query, keys, values, counts):
    total = keys.shape[0]
    place = lax.broadcasted_iota(jnp.int32, (1, total), 1)
    valid = place < TEXT
    for patch in range(NPATCH):
        begin = TEXT + patch * PATCH_TOK
        valid |= (place >= begin) & (place < begin + counts[patch])
    bias = jnp.where(valid, 0.0, -1e30)
    ones = jnp.ones((total, HD), BF16)
    outs = []
    for head in range(keys.shape[1] // HD):
        cols = slice(head * HD, (head + 1) * HD)
        scores = lax.dot_general(
            query[:, cols], keys[:, cols], (((1,), (1,)), ((), ())), preferred_element_type=F32
        )
        scores = scores + bias
        expo = jnp.exp2(scores - jnp.max(scores, axis=-1, keepdims=True)).astype(BF16)
        out = project(expo, jnp.concatenate([values[:, cols], ones], axis=1))
        outs.append((out[:, :HD] / out[:, HD:]).astype(BF16))
    return jnp.concatenate(outs, axis=1)


def attend(begin, sizes, counts, query, keys, values, w_out, pieces=(), mods=None):
    count, model = sum(sizes), w_out.shape[1]
    keep = len(pieces) > 0
    n = len(pieces)

    def kernel(counts, query, keys, values, w_out, *refs):
        out = attended(query[begin : begin + count, :], keys, values, counts)
        mixed = project(out, w_out[...])
        if keep:
            rows = jnp.concatenate([p[...] for p in refs[:n]], axis=0)
            mixed = rows.astype(F32) + refs[n][2:3] * mixed
        place = 0
        for ref, size in zip(refs[-len(sizes) :], sizes):
            ref[...] = mixed[place : place + size].astype(ref.dtype)
            place += size

    extra = (*pieces, mods) if keep else ()
    return pl.pallas_call(
        kernel,
        in_specs=[SMEM] + [VMEM] * (4 + len(extra)),
        out_specs=[VMEM] * len(sizes),
        out_shape=[in_vmem((size, model), F32 if keep else BF16) for size in sizes],
        compiler_params=limit(16),
        cost_estimate=cost(2 * 256 * query.shape[1] * (2 * keys.shape[0] + model)),
        name="attend",
    )(counts, held(query), held(keys), held(values), held(w_out), *extra)


def combine_kernel(base, received, mods, out):
    out[...] = (base[...] + mods[2:3] * received[...].astype(F32)).astype(BF16)


def combine(base, received, mods):
    return pl.pallas_call(
        combine_kernel,
        in_specs=[VMEM] * 3,
        out_specs=VMEM,
        out_shape=in_vmem(received.shape, BF16),
        compiler_params=limit(6),
        name="combine",
    )(held(base), held(received), mods)


def on_device(
    patches, patch_index, step_index, counts, modulation, qk_gain, w_qkv, w_out, cache_k, cache_v
):
    weights = w_qkv[0]
    both = ("section", "cfg")
    swap = [(2 * s + c, 2 * s + 1 - c) for s in range(SECTIONS) for c in range(2)]
    shift = [
        (2 * s + c, 2 * ((s + 1) % SECTIONS) + (c if s % 2 == 0 else 1 - c))
        for s in range(SECTIONS)
        for c in range(2)
    ]

    def exchange(block):
        return lax.ppermute(block, both, swap)

    def move(block):
        return lax.ppermute(block, both, shift)

    own = patches[0]
    early = lax.ppermute(own, both, [p for p in swap if p[0] // 2 % 2 == 0])
    query, copied, mods, mods_next, gains, proj, keys, values = opening(
        patch_index, step_index, own, jnp.transpose(modulation[0], (1, 0, 2)), qk_gain[0], weights,
        w_out[0], cache_k[0], cache_v[0],
    )
    late = lax.ppermute(copied, both, [p for p in swap if p[0] // 2 % 2 == 1])
    query_other, keys, values = qkv(
        0, 1, patch_index, (early, late), mods, gains, weights, keys, values, either=True
    )
    begin = 0
    got = []
    for size in MID:
        got.append(exchange(attend(begin, (size,), counts, query_other, keys, values, proj)[0]))
        begin += size
    base = attend(0, MID, counts, query, keys, values, proj, (copied,), mods)
    own = [move(combine(b, g, mods)) for b, g in zip(base, got)]

    mods = mods_next
    other = [exchange(block) for block in own]
    query, keys, values = qkv(1, 0, patch_index, own, mods, gains, weights, keys, values)
    query_other, keys, values = qkv(1, 1, patch_index, other, mods, gains, weights, keys, values)
    one = attend(0, LAST[:1], counts, query, keys, values, proj)
    two = attend(LAST[0], LAST[1:], counts, query, keys, values, proj)
    got = [exchange(block) for block in (*one, *two)]
    base = attend(0, LAST, counts, query_other, keys, values, proj, other, mods)
    done = [move(combine(b, g, mods)) for b, g in zip(base, got)]
    return jnp.concatenate(done, axis=0)[None]


def solution(mesh):
    in_specs = (
        P("section", "cfg", None),
        P(),
        P(),
        P(),
        P("section", None, None, None),
        P("section", None, None),
        P("section", None, None, "cfg"),
        P("section", "cfg", None),
        P("section", None, "cfg"),
        P("section", None, "cfg"),
    )
    out_specs = P("section", "cfg", None)
    return jax.shard_map(
        on_device, mesh=mesh, in_specs=in_specs, out_specs=out_specs, check_vma=False
    )
```

```python
import jax
import jax.numpy as jnp
from jax import lax
from jax.experimental import pallas as pl
from jax.experimental.pallas import tpu as pltpu
from jax.sharding import PartitionSpec as P

HD = 128
PATCH_TOK = 384
NPATCH = 4
TEXT = 256
SECTIONS = 64
BF16 = jnp.bfloat16
F32 = jnp.float32
VMEM = pl.BlockSpec(memory_space=pltpu.VMEM)
SMEM = pl.BlockSpec(memory_space=pltpu.SMEM)
HBM = pl.BlockSpec(memory_space=pltpu.HBM)
LOOSE = pl.BlockSpec(memory_space=pl.ANY)
MIB = 1024 * 1024
QUERY_SCALE = HD ** (-0.5) * 1.4426950408889634
PARTS = (96, 96)


def held(array):
    return pltpu.with_memory_space_constraint(array, pltpu.VMEM)


def far(array):
    return pltpu.with_memory_space_constraint(array, pltpu.HBM)


def in_vmem(shape, dtype):
    return pltpu.VMEM(shape, dtype)


def loose(shape, dtype):
    return jax.ShapeDtypeStruct(shape, dtype)


def modulated(rows, mods):
    wide = rows.astype(F32)
    mean = jnp.mean(wide, axis=-1, keepdims=True)
    centred = wide - mean
    spread = jnp.mean(centred * centred, axis=-1, keepdims=True)
    normed = centred * lax.rsqrt(spread + 1e-06)
    return (normed * (1.0 + mods[1:2]) + mods[0:1]).astype(BF16)


def head_norm(proj, gain):
    parts = []
    for head in range(proj.shape[1] // HD):
        x = proj[:, head * HD : (head + 1) * HD]
        scale = lax.rsqrt(jnp.mean(x * x, axis=-1, keepdims=True) + 1e-06)
        parts.append((x * scale * gain).astype(BF16))
    return jnp.concatenate(parts, axis=1)


def project(hidden, weights):
    return jnp.dot(hidden, weights, preferred_element_type=F32)


def limit(mib):
    return pltpu.CompilerParams(vmem_limit_bytes=mib * MIB)


def cost(flops):
    del flops
    return pl.CostEstimate(flops=1, bytes_accessed=1, transcendentals=0)


def first_row(tick, side, patch_index, half):
    section, group = lax.axis_index("section"), lax.axis_index("cfg")
    source = lax.rem(section + SECTIONS - tick, SECTIONS)
    swapped = 0 if tick == 0 else 1 - lax.rem(section, 2)
    which = lax.rem(group + swapped + side, 2)
    return pl.multiple_of(TEXT + patch_index[source] * PATCH_TOK + which * half, 32)


def projections(hidden, gains, weights, waits, put_key, put_value, query):
    waits[0]()
    put_key(head_norm(project(hidden, weights[1]), gains[1:2]))
    waits[1]()
    put_value(project(hidden, weights[2]).astype(BF16))
    waits[2]()
    query[...] = head_norm(project(hidden, weights[0]), gains[0:1] * QUERY_SCALE)


def selected(modulation, step):
    at = lax.broadcasted_iota(jnp.int32, (modulation.shape[1], 1), 0) == step
    rows = [
        jnp.sum(jnp.where(at, modulation[i].astype(F32), 0.0), axis=0, keepdims=True)
        for i in range(modulation.shape[0])
    ]
    return jnp.concatenate(rows, axis=0)


def open_kernel(
    patch_far, step_far, rows_far, modulation_far, gains_far, w_qkv_far, w_out_far, keys_far, values_far,
    query, rows, upper, lower, mods_now, mods_next, gains, w_qkv, w_out, keys, values,
    modulation, patch_index, step_index, sems, more,
):
    pairs = [
        (patch_far, patch_index),
        (step_far, step_index),
        (gains_far, gains),
        (modulation_far, modulation),
        (rows_far, rows),
        (keys_far, keys),
        (values_far, values),
        (w_out_far, w_out),
    ]
    others = [pltpu.make_async_copy(a, b, more.at[i]) for i, (a, b) in enumerate(pairs)]
    for copy in others[:5]:
        copy.start()
    copies = [pltpu.make_async_copy(w_qkv_far.at[i], w_qkv.at[i], sems.at[i]) for i in (1, 2, 0)]
    for copy in copies + others[5:]:
        copy.start()
    section = lax.axis_index("section")
    for copy in others[:4]:
        copy.wait()
    mods = selected(modulation, step_index[section])
    mods_now[...] = mods
    mods_next[...] = selected(modulation, step_index[lax.rem(section + SECTIONS - 1, SECTIONS)])
    others[4].wait()
    upper[...] = rows[: upper.shape[0], :]
    lower[...] = rows[upper.shape[0] :, :]
    hidden = modulated(rows[...], mods)
    here = pl.ds(first_row(0, 0, patch_index, rows.shape[0]), rows.shape[0])

    def put_key(fresh):
        others[5].wait()
        keys[here, :] = fresh

    def put_value(fresh):
        others[6].wait()
        values[here, :] = fresh

    projections(hidden, gains[...], w_qkv, [c.wait for c in copies], put_key, put_value, query)
    others[7].wait()


def opening(patch_index, step_index, rows, modulation, gains, w_qkv, w_out, keys, values):
    model = rows.shape[1]
    return pl.pallas_call(
        open_kernel,
        in_specs=[HBM] * 9,
        out_specs=[VMEM] * 11,
        out_shape=[
            in_vmem((rows.shape[0], keys.shape[1]), BF16),
            in_vmem(rows.shape, BF16),
            loose((PARTS[0], model), BF16),
            loose((PARTS[1], model), BF16),
            loose((3, model), F32),
            loose((3, model), F32),
            loose(gains.shape, F32),
            in_vmem(w_qkv.shape, BF16),
            in_vmem(w_out.shape, BF16),
            in_vmem(keys.shape, BF16),
            in_vmem(values.shape, BF16),
        ],
        scratch_shapes=[
            pltpu.VMEM(modulation.shape, BF16),
            pltpu.SMEM(patch_index.shape, jnp.int32),
            pltpu.SMEM(step_index.shape, jnp.int32),
            pltpu.SemaphoreType.DMA((3,)),
            pltpu.SemaphoreType.DMA((8,)),
        ],
        compiler_params=limit(16),
        cost_estimate=cost(2 * w_qkv.size * 256),
        name="opening",
    )(*map(far, (patch_index, step_index, rows, modulation, gains, w_qkv, w_out, keys, values)))


def on_parity(parity, body):
    pl.when(lax.rem(lax.axis_index("section"), 2) == parity)(body)


def qkv(parity, tick, side, patch_index, pieces, mods, gains, w_qkv, keys, values, after=()):
    count, width = sum(p.shape[0] for p in pieces), keys.shape[1]
    n = len(pieces)

    def kernel(patch_index, *refs):
        parts, (mods, gains, w_qkv, _, _) = refs[:n], refs[n : n + 5]
        query, keys, values = refs[-3:]

        def body():
            rows = [p[...] for p in parts]
            hidden = modulated(rows[0] if n == 1 else jnp.concatenate(rows, axis=0), mods[...])
            here = pl.ds(first_row(tick, side, patch_index, count), count)

            def put_key(fresh):
                keys[here, :] = fresh

            def put_value(fresh):
                values[here, :] = fresh

            none = [lambda: None] * 3
            projections(hidden, gains[...], w_qkv, none, put_key, put_value, query)

        on_parity(parity, body)

    return pl.pallas_call(
        kernel,
        in_specs=[SMEM] + [VMEM] * (n + 5) + [LOOSE] * len(after),
        out_specs=[VMEM] * 3,
        out_shape=[in_vmem((count, width), BF16), in_vmem(keys.shape, BF16), in_vmem(values.shape, BF16)],
        input_output_aliases={n + 4: 1, n + 5: 2},
        compiler_params=limit(16),
        cost_estimate=cost(2 * w_qkv.size * 256),
        name="qkv",
    )(patch_index, *pieces, mods, gains, held(w_qkv), held(keys), held(values), *after)


def attended(query, keys, values, counts):
    total = keys.shape[0]
    place = lax.broadcasted_iota(jnp.int32, (1, total), 1)
    valid = place < TEXT
    for patch in range(NPATCH):
        begin = TEXT + patch * PATCH_TOK
        valid |= (place >= begin) & (place < begin + counts[patch])
    bias = jnp.where(valid, 0.0, -1e30)
    ones = jnp.ones((total, HD), BF16)
    outs = []
    for head in range(keys.shape[1] // HD):
        cols = slice(head * HD, (head + 1) * HD)
        scores = lax.dot_general(
            query[:, cols], keys[:, cols], (((1,), (1,)), ((), ())), preferred_element_type=F32
        )
        scores = scores + bias
        expo = jnp.exp2(scores - jnp.max(scores, axis=-1, keepdims=True)).astype(BF16)
        out = project(expo, jnp.concatenate([values[:, cols], ones], axis=1))
        outs.append((out[:, :HD] / out[:, HD:]).astype(BF16))
    return jnp.concatenate(outs, axis=1)


def attend(parity, begin, sizes, counts, query, keys, values, w_out, pieces=(), mods=None, after=()):
    count, model = sum(sizes), w_out.shape[1]
    keep = len(pieces) > 0
    n = len(pieces)

    def kernel(counts, query, keys, values, w_out, *refs):
        def body():
            out = attended(query[begin : begin + count, :], keys, values, counts)
            mixed = project(out, w_out[...])
            if keep:
                rows = jnp.concatenate([p[...] for p in refs[:n]], axis=0)
                mixed = rows.astype(F32) + refs[n][2:3] * mixed
            place = 0
            for ref, size in zip(refs[-len(sizes) :], sizes):
                ref[...] = mixed[place : place + size].astype(ref.dtype)
                place += size

        on_parity(parity, body)

    extra = (*pieces, mods) if keep else ()
    return pl.pallas_call(
        kernel,
        in_specs=[SMEM] + [VMEM] * (4 + len(extra)) + [LOOSE] * len(after),
        out_specs=[VMEM] * len(sizes),
        out_shape=[in_vmem((size, model), F32 if keep else BF16) for size in sizes],
        compiler_params=limit(16),
        cost_estimate=cost(2 * 256 * query.shape[1] * (2 * keys.shape[0] + model)),
        name="attend",
    )(counts, held(query), held(keys), held(values), held(w_out), *extra, *after)


def combine(parity, base, received, mods, after=()):
    def kernel(base, received, mods, *refs):
        def body():
            refs[-1][...] = (base[...] + mods[2:3] * received[...].astype(F32)).astype(BF16)

        on_parity(parity, body)

    return pl.pallas_call(
        kernel,
        in_specs=[VMEM] * 3 + [LOOSE] * len(after),
        out_specs=VMEM,
        out_shape=in_vmem(received.shape, BF16),
        compiler_params=limit(6),
        cost_estimate=cost(1000000),
        name="combine",
    )(held(base), held(received), mods, *after)


def relay(parity, blocks, after):
    n = len(blocks)

    def kernel(*refs):
        def body():
            for source, target in zip(refs[:n], refs[-n:]):
                target[...] = source[...]

        on_parity(parity, body)

    return pl.pallas_call(
        kernel,
        in_specs=[VMEM] * n + [LOOSE] * len(after),
        out_specs=[VMEM] * n,
        out_shape=[in_vmem(b.shape, BF16) for b in blocks],
        compiler_params=limit(6),
        cost_estimate=cost(0),
        name="relay",
    )(*blocks, *after)


def on_device(
    patches, patch_index, step_index, counts, modulation, qk_gain, w_qkv, w_out, cache_k, cache_v
):
    both = ("section", "cfg")
    swap, shift = ([], []), ([], [])
    for s in range(SECTIONS):
        for c in range(2):
            swap[s % 2].append((2 * s + c, 2 * s + 1 - c))
            shift[s % 2].append((2 * s + c, 2 * ((s + 1) % SECTIONS) + (c if s % 2 == 0 else 1 - c)))

    def exchange(parity, block):
        return lax.ppermute(block, both, swap[parity])

    def move(parity, block):
        return lax.ppermute(block, both, shift[parity])

    def attention(parity, sent_query, kept_query, kept_rows, keys, values, mods, after, wait=((), ()), ahead=(), keep_first=False):
        def keep(after):
            return attend(
                parity, 0, PARTS, counts, kept_query, keys, values, proj, kept_rows, mods, (*after, *wait[0])
            )

        if keep_first:
            base = keep(after)
            sent = attend(parity, 0, PARTS, counts, sent_query, keys, values, proj, after=base)
            after = tuple(sent)
        else:
            sent, begin = [], 0
            for size in PARTS:
                part = attend(parity, begin, (size,), counts, sent_query, keys, values, proj, after=after)
                after, begin = tuple(part), begin + size
                sent += part
            base = keep(after)
        got = [exchange(parity, part) for part in sent]
        if ahead:
            ahead = relay(parity, ahead, base)
        moved, after = [], (*after, *wait[1], *ahead)
        for b, g in zip(base, got):
            done = combine(parity, b, g, mods, after)
            after = (done,)
            moved.append(move(parity, done))
        return moved, after, ahead

    own = patches[0]
    even = exchange(0, own)
    query, copied, upper, lower, mods, mods_next, gains, weights, proj, keys, values = opening(
        patch_index, step_index, own, jnp.transpose(modulation[0], (1, 0, 2)), qk_gain[0], w_qkv[0],
        w_out[0], cache_k[0], cache_v[0],
    )
    odd = (exchange(1, upper), exchange(1, lower))
    moved, after = [(), ()], ()
    for parity in (0, 1):
        rows = (even,) if parity == 0 else odd
        query_other, keys, values = qkv(
            parity, 0, 1, patch_index, rows, mods, gains, weights, keys, values, after
        )
        moved[parity], after, ahead = attention(
            parity, query_other, query, (copied,), keys, values, mods, after, ahead=moved[1 - parity]
        )

    mods, last = mods_next, [(), ()]
    others = [[exchange(0, block) for block in moved[1]], [exchange(1, block) for block in ahead]]
    for parity in (1, 0):
        own, other = moved[1 - parity], others[parity]
        query, keys, values = qkv(parity, 1, 0, patch_index, own, mods, gains, weights, keys, values, after)
        query_other, keys, values = qkv(parity, 1, 1, patch_index, other, mods, gains, weights, keys, values)
        last[parity], after, _ = attention(
            parity, query, query_other, other, keys, values, mods, after, (last[1 - parity][:1], last[1 - parity][1:]),
            keep_first=parity == 1,
        )
    return jnp.concatenate([a + b for a, b in zip(*last)], axis=0)[None]


def solution(mesh):
    in_specs = (
        P("section", "cfg", None),
        P(),
        P(),
        P(),
        P("section", None, None, None),
        P("section", None, None),
        P("section", None, None, "cfg"),
        P("section", "cfg", None),
        P("section", None, "cfg"),
        P("section", None, "cfg"),
    )
    out_specs = P("section", "cfg", None)
    return jax.shard_map(
        on_device, mesh=mesh, in_specs=in_specs, out_specs=out_specs, check_vma=False
    )
```

```python
import jax
import jax.numpy as jnp
from jax import lax
from jax.experimental import pallas as pl
from jax.experimental.pallas import tpu as pltpu
from jax.sharding import PartitionSpec as P

HD = 128
PATCH_TOK = 384
NPATCH = 4
TEXT = 256
SECTIONS = 64
BF16 = jnp.bfloat16
F32 = jnp.float32
VMEM = pl.BlockSpec(memory_space=pltpu.VMEM)
SMEM = pl.BlockSpec(memory_space=pltpu.SMEM)
HBM = pl.BlockSpec(memory_space=pltpu.HBM)
MIB = 1024 * 1024
QUERY_SCALE = HD ** (-0.5) * 1.4426950408889634
BLOCK = 1536
MID = (96, 96)
LAST = (64, 64, 64)


def held(array):
    return pltpu.with_memory_space_constraint(array, pltpu.VMEM)


def far(array):
    return pltpu.with_memory_space_constraint(array, pltpu.HBM)


def in_vmem(shape, dtype):
    return pltpu.VMEM(shape, dtype)


def loose(shape, dtype):
    return jax.ShapeDtypeStruct(shape, dtype)


def modulated(rows, mods):
    wide = rows.astype(F32)
    mean = jnp.mean(wide, axis=-1, keepdims=True)
    centred = wide - mean
    spread = jnp.mean(centred * centred, axis=-1, keepdims=True)
    normed = centred * lax.rsqrt(spread + 1e-06)
    return (normed * (1.0 + mods[1:2]) + mods[0:1]).astype(BF16)


def head_norm(proj, gain):
    parts = []
    for head in range(proj.shape[1] // HD):
        x = proj[:, head * HD : (head + 1) * HD]
        scale = lax.rsqrt(jnp.mean(x * x, axis=-1, keepdims=True) + 1e-06)
        parts.append((x * scale * gain).astype(BF16))
    return jnp.concatenate(parts, axis=1)


def project(hidden, weights):
    return jnp.dot(hidden, weights, preferred_element_type=F32)


def limit(mib):
    return pltpu.CompilerParams(vmem_limit_bytes=mib * MIB)


def cost(flops):
    return pl.CostEstimate(flops=int(flops), bytes_accessed=1000000, transcendentals=0)


def first_row(tick, side, patch_index, half):
    section, group = lax.axis_index("section"), lax.axis_index("cfg")
    source = lax.rem(section + SECTIONS - tick, SECTIONS)
    swapped = 0 if tick == 0 else 1 - lax.rem(section, 2)
    which = lax.rem(group + swapped + side, 2)
    return pl.multiple_of(TEXT + patch_index[source] * PATCH_TOK + which * half, 32)


def projections(hidden, gains, weights, waits, put_key, put_value, query):
    waits[0]()
    put_key(head_norm(project(hidden, weights[1]), gains[1:2]))
    waits[1]()
    put_value(project(hidden, weights[2]).astype(BF16))
    waits[2]()
    query[...] = head_norm(project(hidden, weights[0]), gains[0:1] * QUERY_SCALE)


def selected(modulation, step):
    at = lax.broadcasted_iota(jnp.int32, (modulation.shape[1], 1), 0) == step
    rows = [
        jnp.sum(jnp.where(at, modulation[i].astype(F32), 0.0), axis=0, keepdims=True)
        for i in range(modulation.shape[0])
    ]
    return jnp.concatenate(rows, axis=0)


def open_kernel(
    patch_far, step_far, rows_far, modulation_far, gains_far, w_qkv_far, w_out_far, keys_far, values_far,
    query, rows, upper, lower, mods_now, mods_next, gains, w_qkv, w_out, keys, values,
    modulation, patch_index, step_index, sems, more,
):
    pairs = [
        (patch_far, patch_index),
        (step_far, step_index),
        (gains_far, gains),
        (modulation_far, modulation),
        (rows_far, rows),
        (keys_far, keys),
        (values_far, values),
        (w_out_far, w_out),
    ]
    others = [pltpu.make_async_copy(a, b, more.at[i]) for i, (a, b) in enumerate(pairs)]
    for copy in others[:5]:
        copy.start()
    copies = [pltpu.make_async_copy(w_qkv_far.at[i], w_qkv.at[i], sems.at[i]) for i in (1, 2, 0)]
    for copy in copies + others[5:]:
        copy.start()
    section = lax.axis_index("section")
    for copy in others[:4]:
        copy.wait()
    mods = selected(modulation, step_index[section])
    mods_now[...] = mods
    mods_next[...] = selected(modulation, step_index[lax.rem(section + SECTIONS - 1, SECTIONS)])
    others[4].wait()
    upper[...] = rows[: upper.shape[0], :]
    lower[...] = rows[upper.shape[0] :, :]
    hidden = modulated(rows[...], mods)
    here = pl.ds(first_row(0, 0, patch_index, rows.shape[0]), rows.shape[0])

    def put_key(fresh):
        others[5].wait()
        keys[here, :] = fresh

    def put_value(fresh):
        others[6].wait()
        values[here, :] = fresh

    projections(hidden, gains[...], w_qkv, [c.wait for c in copies], put_key, put_value, query)
    others[7].wait()


def opening(patch_index, step_index, rows, modulation, gains, w_qkv, w_out, keys, values):
    model = rows.shape[1]
    return pl.pallas_call(
        open_kernel,
        in_specs=[HBM] * 9,
        out_specs=[VMEM] * 11,
        out_shape=[
            in_vmem((rows.shape[0], keys.shape[1]), BF16),
            in_vmem(rows.shape, BF16),
            loose((MID[0], model), BF16),
            loose((MID[1], model), BF16),
            loose((3, model), F32),
            loose((3, model), F32),
            loose(gains.shape, F32),
            in_vmem(w_qkv.shape, BF16),
            in_vmem(w_out.shape, BF16),
            in_vmem(keys.shape, BF16),
            in_vmem(values.shape, BF16),
        ],
        scratch_shapes=[
            pltpu.VMEM(modulation.shape, BF16),
            pltpu.SMEM(patch_index.shape, jnp.int32),
            pltpu.SMEM(step_index.shape, jnp.int32),
            pltpu.SemaphoreType.DMA((3,)),
            pltpu.SemaphoreType.DMA((8,)),
        ],
        compiler_params=limit(16),
        cost_estimate=cost(2 * w_qkv.size * 256),
        name="opening",
    )(*map(far, (patch_index, step_index, rows, modulation, gains, w_qkv, w_out, keys, values)))


def qkv(tick, side, patch_index, pairs, mods, gains, w_qkv, keys, values):
    count, width = sum(p[0].shape[0] for p in pairs), keys.shape[1]
    n = sum(map(len, pairs))

    def kernel(patch_index, *refs):
        parts, (mods, gains, w_qkv, _, _) = refs[:n], refs[n : n + 5]
        query, keys, values = refs[n + 5 :]
        rows, place = [], 0
        for p in pairs:
            one, *two = [ref[...] for ref in parts[place : place + len(p)]]
            rows.append(one + jnp.concatenate(two, axis=0) if two else one)
            place += len(p)
        hidden = modulated(rows[0] if len(pairs) == 1 else jnp.concatenate(rows, axis=0), mods[...])
        here = pl.ds(first_row(tick, side, patch_index, count), count)

        def put_key(fresh):
            keys[here, :] = fresh

        def put_value(fresh):
            values[here, :] = fresh

        none = [lambda: None] * 3
        projections(hidden, gains[...], w_qkv, none, put_key, put_value, query)

    return pl.pallas_call(
        kernel,
        in_specs=[SMEM] + [VMEM] * (n + 5),
        out_specs=[VMEM] * 3,
        out_shape=[in_vmem((count, width), BF16), in_vmem(keys.shape, BF16), in_vmem(values.shape, BF16)],
        input_output_aliases={n + 4: 1, n + 5: 2},
        compiler_params=limit(16),
        cost_estimate=cost(2 * w_qkv.size * 256),
        name="qkv",
    )(patch_index, *(a for p in pairs for a in p), mods, gains, held(w_qkv), held(keys), held(values))


def attended(query, keys, values, counts):
    total = keys.shape[0]
    place = lax.broadcasted_iota(jnp.int32, (1, total), 1)
    valid = place < TEXT
    for patch in range(NPATCH):
        begin = TEXT + patch * PATCH_TOK
        valid |= (place >= begin) & (place < begin + counts[patch])
    bias = jnp.where(valid, 0.0, -1e30)
    ones = jnp.ones((total, HD), BF16)
    outs = []
    for head in range(keys.shape[1] // HD):
        cols = slice(head * HD, (head + 1) * HD)
        scores = lax.dot_general(
            query[:, cols], keys[:, cols], (((1,), (1,)), ((), ())), preferred_element_type=F32
        )
        scores = scores + bias
        expo = jnp.exp2(scores - jnp.max(scores, axis=-1, keepdims=True)).astype(BF16)
        out = project(expo, jnp.concatenate([values[:, cols], ones], axis=1))
        outs.append((out[:, :HD] / out[:, HD:]).astype(BF16))
    return jnp.concatenate(outs, axis=1)


def attend(begin, sizes, counts, query, keys, values, w_out, pieces=(), mods=None):
    count, model = sum(sizes), w_out.shape[1]
    keep = len(pieces) > 0
    n = len(pieces)

    def kernel(counts, query, keys, values, w_out, *refs):
        out, outs = refs[-1], refs[-1 - len(sizes) : -1]
        out[...] = attended(query[begin : begin + count, :], keys, values, counts)

        def columns(i, carry):
            cols = pl.ds(pl.multiple_of(i * BLOCK, BLOCK), BLOCK)
            mixed = project(out[...], w_out[:, cols])
            if keep:
                rows = jnp.concatenate([p[:, cols] for p in refs[:n]], axis=0)
                mixed = rows.astype(F32) + refs[n][2:3, cols] * mixed
            place = 0
            for ref, size in zip(outs, sizes):
                ref[:, cols] = mixed[place : place + size].astype(ref.dtype)
                place += size
            return carry

        lax.fori_loop(0, model // BLOCK, columns, 0)

    extra = (*pieces, mods) if keep else ()
    return pl.pallas_call(
        kernel,
        in_specs=[SMEM] + [VMEM] * (4 + len(extra)),
        out_specs=[VMEM] * len(sizes),
        out_shape=[in_vmem((size, model), F32 if keep else BF16) for size in sizes],
        scratch_shapes=[pltpu.VMEM((count, query.shape[1]), BF16)],
        compiler_params=limit(16),
        cost_estimate=cost(2 * 256 * query.shape[1] * (2 * keys.shape[0] + model)),
        name="attend",
    )(counts, held(query), held(keys), held(values), held(w_out), *extra)


def combine_kernel(base, received, mods, out):
    out[...] = (base[...] + mods[2:3] * received[...].astype(F32)).astype(BF16)


def combine(base, received, mods):
    return pl.pallas_call(
        combine_kernel,
        in_specs=[VMEM] * 3,
        out_specs=VMEM,
        out_shape=in_vmem(received.shape, BF16),
        compiler_params=limit(6),
        name="combine",
    )(held(base), held(received), mods)


def on_device(
    patches, patch_index, step_index, counts, modulation, qk_gain, w_qkv, w_out, cache_k, cache_v
):
    both = ("section", "cfg")
    swap = [(2 * s + c, 2 * s + 1 - c) for s in range(SECTIONS) for c in range(2)]
    shift = [
        (2 * s + c, 2 * ((s + 1) % SECTIONS) + (c if s % 2 == 0 else 1 - c))
        for s in range(SECTIONS)
        for c in range(2)
    ]

    def exchange(block):
        return lax.ppermute(block, both, swap)

    def move(block):
        return lax.ppermute(block, both, shift)

    own = patches[0]
    early = lax.ppermute(own, both, [p for p in swap if p[0] // 2 % 2 == 0])
    query, copied, upper, lower, mods, mods_next, gains, weights, proj, keys, values = opening(
        patch_index, step_index, own, jnp.transpose(modulation[0], (1, 0, 2)), qk_gain[0], w_qkv[0],
        w_out[0], cache_k[0], cache_v[0],
    )
    late = [lax.ppermute(piece, both, [p for p in swap if p[0] // 2 % 2 == 1]) for piece in (upper, lower)]
    query_other, keys, values = qkv(
        0, 1, patch_index, [(early, *late)], mods, gains, weights, keys, values
    )
    begin = 0
    got = []
    for size in MID:
        got.append(exchange(attend(begin, (size,), counts, query_other, keys, values, proj)[0]))
        begin += size
    base = attend(0, MID, counts, query, keys, values, proj, (copied,), mods)
    own = [move(combine(b, g, mods)) for b, g in zip(base, got)]

    mods = mods_next
    other = [exchange(block) for block in own]
    query, keys, values = qkv(1, 0, patch_index, [(p,) for p in own], mods, gains, weights, keys, values)
    query_other, keys, values = qkv(1, 1, patch_index, [(p,) for p in other], mods, gains, weights, keys, values)
    one = attend(0, LAST[:1], counts, query, keys, values, proj)
    two = attend(LAST[0], LAST[1:], counts, query, keys, values, proj)
    got = [exchange(block) for block in (*one, *two)]
    base = attend(0, LAST, counts, query_other, keys, values, proj, other, mods)
    done = [move(combine(b, g, mods)) for b, g in zip(base, got)]
    return jnp.concatenate(done, axis=0)[None]


def solution(mesh):
    in_specs = (
        P("section", "cfg", None),
        P(),
        P(),
        P(),
        P("section", None, None, None),
        P("section", None, None),
        P("section", None, None, "cfg"),
        P("section", "cfg", None),
        P("section", None, "cfg"),
        P("section", None, "cfg"),
    )
    out_specs = P("section", "cfg", None)
    return jax.shard_map(
        on_device, mesh=mesh, in_specs=in_specs, out_specs=out_specs, check_vma=False
    )
```

```python
import jax
import jax.numpy as jnp
from jax import lax
from jax.experimental import pallas as pl
from jax.experimental.pallas import tpu as pltpu
from jax.sharding import PartitionSpec as P

HD = 128
PATCH_TOK = 384
NPATCH = 4
TEXT = 256
SECTIONS = 64
BF16 = jnp.bfloat16
F32 = jnp.float32
VMEM = pl.BlockSpec(memory_space=pltpu.VMEM)
SMEM = pl.BlockSpec(memory_space=pltpu.SMEM)
HBM = pl.BlockSpec(memory_space=pltpu.HBM)
LOOSE = pl.BlockSpec(memory_space=pl.ANY)
MIB = 1024 * 1024
QUERY_SCALE = HD ** (-0.5) * 1.4426950408889634
BLOCK = 1536
MID = (96, 96)
LAST = (80, 64, 48)


def held(array):
    return pltpu.with_memory_space_constraint(array, pltpu.VMEM)


def far(array):
    return pltpu.with_memory_space_constraint(array, pltpu.HBM)


def in_vmem(shape, dtype):
    return pltpu.VMEM(shape, dtype)


def loose(shape, dtype):
    return jax.ShapeDtypeStruct(shape, dtype)


def modulated(rows, mods):
    wide = rows.astype(F32)
    mean = jnp.mean(wide, axis=-1, keepdims=True)
    centred = wide - mean
    spread = jnp.mean(centred * centred, axis=-1, keepdims=True)
    normed = centred * lax.rsqrt(spread + 1e-06)
    return (normed * (1.0 + mods[1:2]) + mods[0:1]).astype(BF16)


def head_norm(proj, gain):
    parts = []
    for head in range(proj.shape[1] // HD):
        x = proj[:, head * HD : (head + 1) * HD]
        scale = lax.rsqrt(jnp.mean(x * x, axis=-1, keepdims=True) + 1e-06)
        parts.append((x * scale * gain).astype(BF16))
    return jnp.concatenate(parts, axis=1)


def project(hidden, weights):
    return jnp.dot(hidden, weights, preferred_element_type=F32)


def limit(mib):
    return pltpu.CompilerParams(vmem_limit_bytes=mib * MIB)


def cost(flops):
    return pl.CostEstimate(flops=int(flops), bytes_accessed=1000000, transcendentals=0)


def first_row(tick, side, patch_index, half):
    section, group = lax.axis_index("section"), lax.axis_index("cfg")
    source = lax.rem(section + SECTIONS - tick, SECTIONS)
    swapped = 0 if tick == 0 else 1 - lax.rem(section, 2)
    which = lax.rem(group + swapped + side, 2)
    return pl.multiple_of(TEXT + patch_index[source] * PATCH_TOK + which * half, 32)


def projections(hidden, gains, weights, waits, put_key, put_value, query):
    waits[0]()
    put_key(head_norm(project(hidden, weights[1]), gains[1:2]))
    waits[1]()
    put_value(project(hidden, weights[2]).astype(BF16))
    waits[2]()
    query[...] = head_norm(project(hidden, weights[0]), gains[0:1] * QUERY_SCALE)


def selected(modulation, step):
    at = lax.broadcasted_iota(jnp.int32, (modulation.shape[1], 1), 0) == step
    rows = [
        jnp.sum(jnp.where(at, modulation[i].astype(F32), 0.0), axis=0, keepdims=True)
        for i in range(modulation.shape[0])
    ]
    return jnp.concatenate(rows, axis=0)


def open_kernel(
    patch_far, step_far, rows_far, modulation_far, gains_far, w_qkv_far, w_out_far, keys_far, values_far,
    query, rows, upper, lower, mods_now, mods_next, gains, w_qkv, w_out, keys, values,
    modulation, patch_index, step_index, sems, more,
):
    pairs = [
        (patch_far, patch_index),
        (step_far, step_index),
        (gains_far, gains),
        (modulation_far, modulation),
        (rows_far, rows),
        (keys_far, keys),
        (values_far, values),
        (w_out_far, w_out),
    ]
    others = [pltpu.make_async_copy(a, b, more.at[i]) for i, (a, b) in enumerate(pairs)]
    for copy in others[:5]:
        copy.start()
    copies = [pltpu.make_async_copy(w_qkv_far.at[i], w_qkv.at[i], sems.at[i]) for i in (1, 2, 0)]
    for copy in copies + others[5:]:
        copy.start()
    section = lax.axis_index("section")
    for copy in others[:4]:
        copy.wait()
    mods = selected(modulation, step_index[section])
    mods_now[...] = mods
    mods_next[...] = selected(modulation, step_index[lax.rem(section + SECTIONS - 1, SECTIONS)])
    others[4].wait()
    upper[...] = rows[: upper.shape[0], :]
    lower[...] = rows[upper.shape[0] :, :]
    hidden = modulated(rows[...], mods)
    here = pl.ds(first_row(0, 0, patch_index, rows.shape[0]), rows.shape[0])

    def put_key(fresh):
        others[5].wait()
        keys[here, :] = fresh

    def put_value(fresh):
        others[6].wait()
        values[here, :] = fresh

    projections(hidden, gains[...], w_qkv, [c.wait for c in copies], put_key, put_value, query)
    others[7].wait()


def opening(patch_index, step_index, rows, modulation, gains, w_qkv, w_out, keys, values):
    model = rows.shape[1]
    return pl.pallas_call(
        open_kernel,
        in_specs=[HBM] * 9,
        out_specs=[VMEM] * 11,
        out_shape=[
            in_vmem((rows.shape[0], keys.shape[1]), BF16),
            in_vmem(rows.shape, BF16),
            loose((MID[0], model), BF16),
            loose((MID[1], model), BF16),
            loose((3, model), F32),
            loose((3, model), F32),
            loose(gains.shape, F32),
            in_vmem(w_qkv.shape, BF16),
            in_vmem(w_out.shape, BF16),
            in_vmem(keys.shape, BF16),
            in_vmem(values.shape, BF16),
        ],
        scratch_shapes=[
            pltpu.VMEM(modulation.shape, BF16),
            pltpu.SMEM(patch_index.shape, jnp.int32),
            pltpu.SMEM(step_index.shape, jnp.int32),
            pltpu.SemaphoreType.DMA((3,)),
            pltpu.SemaphoreType.DMA((8,)),
        ],
        compiler_params=limit(16),
        cost_estimate=cost(2 * w_qkv.size * 256),
        name="opening",
    )(*map(far, (patch_index, step_index, rows, modulation, gains, w_qkv, w_out, keys, values)))


def qkv(tick, side, patch_index, half, offset, pairs, mods, gains, w_qkv, keys, values, late=False):
    count, width = sum(p[0].shape[0] for p in pairs), keys.shape[1]
    n = sum(map(len, pairs))

    def kernel(patch_index, *refs):
        parts, (mods, gains, w_qkv, _, _) = refs[:n], refs[n : n + 5]
        query, keys, values = refs[n + 5 :]
        rows, place = [], 0
        for p in pairs:
            one, *two = [ref[...] for ref in parts[place : place + len(p)]]
            rows.append(one + jnp.concatenate(two, axis=0) if two else one)
            place += len(p)
        hidden = modulated(rows[0] if len(pairs) == 1 else jnp.concatenate(rows, axis=0), mods[...])
        here = pl.ds(pl.multiple_of(first_row(tick, side, patch_index, half) + offset, 32), count)
        if late:
            query[...] = hidden
        keys[here, :] = head_norm(project(hidden, w_qkv[1]), gains[1:2])
        values[here, :] = project(hidden, w_qkv[2]).astype(BF16)
        if not late:
            query[...] = head_norm(project(hidden, w_qkv[0]), gains[0:1] * QUERY_SCALE)

    return pl.pallas_call(
        kernel,
        in_specs=[SMEM] + [VMEM] * (n + 5),
        out_specs=[VMEM] * 3,
        out_shape=[
            in_vmem((count, pairs[0][0].shape[1] if late else width), BF16),
            in_vmem(keys.shape, BF16),
            in_vmem(values.shape, BF16),
        ],
        input_output_aliases={n + 4: 1, n + 5: 2},
        compiler_params=limit(16),
        cost_estimate=cost(2 * w_qkv.size * 256),
        name="qkv",
    )(patch_index, *(a for p in pairs for a in p), mods, gains, held(w_qkv), held(keys), held(values))


def late_query_kernel(hidden, gains, w_qkv, after, query):
    del after
    query[...] = head_norm(project(hidden[...], w_qkv[0]), gains[0:1] * QUERY_SCALE)


def late_query(hidden, gains, w_qkv, after):
    return pl.pallas_call(
        late_query_kernel,
        in_specs=[VMEM] * 3 + [LOOSE],
        out_specs=VMEM,
        out_shape=in_vmem((hidden.shape[0], w_qkv.shape[2]), BF16),
        compiler_params=limit(16),
        cost_estimate=cost(2 * w_qkv.size * 256 / 3),
        name="late_query",
    )(held(hidden), gains, held(w_qkv), after)


def attended(query, keys, values, counts):
    total = keys.shape[0]
    place = lax.broadcasted_iota(jnp.int32, (1, total), 1)
    valid = place < TEXT
    for patch in range(NPATCH):
        begin = TEXT + patch * PATCH_TOK
        valid |= (place >= begin) & (place < begin + counts[patch])
    bias = jnp.where(valid, 0.0, -1e30)
    ones = jnp.ones((total, HD), BF16)
    outs = []
    for head in range(keys.shape[1] // HD):
        cols = slice(head * HD, (head + 1) * HD)
        scores = lax.dot_general(
            query[:, cols], keys[:, cols], (((1,), (1,)), ((), ())), preferred_element_type=F32
        )
        scores = scores + bias
        expo = jnp.exp2(scores - jnp.max(scores, axis=-1, keepdims=True)).astype(BF16)
        out = project(expo, jnp.concatenate([values[:, cols], ones], axis=1))
        outs.append((out[:, :HD] / out[:, HD:]).astype(BF16))
    return jnp.concatenate(outs, axis=1)


def attend(begin, sizes, counts, query, keys, values, w_out, pieces=(), mods=None):
    count, model = sum(sizes), w_out.shape[1]
    keep = len(pieces) > 0
    queries = query if isinstance(query, tuple) else (query,)
    n, k = len(pieces), len(queries)

    def kernel(counts, *refs):
        query, (keys, values, w_out), refs = refs[:k], refs[k : k + 3], refs[k + 3 :]
        out, outs = refs[-1], refs[-1 - len(sizes) : -1]
        if k == 1:
            rows = query[0][begin : begin + count, :]
        else:
            rows = jnp.concatenate([q[...] for q in query], axis=0)
        out[...] = attended(rows, keys, values, counts)

        def columns(i, carry):
            cols = pl.ds(pl.multiple_of(i * BLOCK, BLOCK), BLOCK)
            mixed = project(out[...], w_out[:, cols])
            if keep:
                rows = jnp.concatenate([p[:, cols] for p in refs[:n]], axis=0)
                mixed = rows.astype(F32) + refs[n][2:3, cols] * mixed
            place = 0
            for ref, size in zip(outs, sizes):
                ref[:, cols] = mixed[place : place + size].astype(ref.dtype)
                place += size
            return carry

        lax.fori_loop(0, model // BLOCK, columns, 0)

    extra = (*pieces, mods) if keep else ()
    return pl.pallas_call(
        kernel,
        in_specs=[SMEM] + [VMEM] * (3 + k + len(extra)),
        out_specs=[VMEM] * len(sizes),
        out_shape=[in_vmem((size, model), F32 if keep else BF16) for size in sizes],
        scratch_shapes=[pltpu.VMEM((count, keys.shape[1]), BF16)],
        compiler_params=limit(16),
        cost_estimate=cost(2 * 256 * keys.shape[1] * (2 * keys.shape[0] + model)),
        name="attend",
    )(counts, *map(held, queries), held(keys), held(values), held(w_out), *extra)


def combine_kernel(base, received, mods, out):
    out[...] = (base[...] + mods[2:3] * received[...].astype(F32)).astype(BF16)


def combine(base, received, mods):
    return pl.pallas_call(
        combine_kernel,
        in_specs=[VMEM] * 3,
        out_specs=VMEM,
        out_shape=in_vmem(received.shape, BF16),
        compiler_params=limit(6),
        name="combine",
    )(held(base), held(received), mods)


def on_device(
    patches, patch_index, step_index, counts, modulation, qk_gain, w_qkv, w_out, cache_k, cache_v
):
    both = ("section", "cfg")
    swap = [(2 * s + c, 2 * s + 1 - c) for s in range(SECTIONS) for c in range(2)]
    shift = [
        (2 * s + c, 2 * ((s + 1) % SECTIONS) + (c if s % 2 == 0 else 1 - c))
        for s in range(SECTIONS)
        for c in range(2)
    ]

    def exchange(block):
        return lax.ppermute(block, both, swap)

    def move(block):
        return lax.ppermute(block, both, shift)

    own = patches[0]
    early = lax.ppermute(own, both, [p for p in swap if p[0] // 2 % 2 == 0])
    query, copied, upper, lower, mods, mods_next, gains, weights, proj, keys, values = opening(
        patch_index, step_index, own, jnp.transpose(modulation[0], (1, 0, 2)), qk_gain[0], w_qkv[0],
        w_out[0], cache_k[0], cache_v[0],
    )
    late = [lax.ppermute(piece, both, [p for p in swap if p[0] // 2 % 2 == 1]) for piece in (upper, lower)]
    query_other, keys, values = qkv(
        0, 1, patch_index, own.shape[0], 0, [(early, *late)], mods, gains, weights, keys, values
    )
    begin = 0
    got = []
    for size in MID:
        got.append(exchange(attend(begin, (size,), counts, query_other, keys, values, proj)[0]))
        begin += size
    base = attend(0, MID, counts, query, keys, values, proj, (copied,), mods)
    own = [move(combine(b, g, mods)) for b, g in zip(base, got)]

    mods = mods_next
    other = [exchange(block) for block in own]
    half = patches.shape[1]
    query, keys, values = qkv(1, 0, patch_index, half, 0, [(p,) for p in own], mods, gains, weights, keys, values)
    query_other, keys, values = qkv(
        1, 1, patch_index, half, 0, [(other[0],)], mods, gains, weights, keys, values
    )
    hidden, keys, values = qkv(
        1, 1, patch_index, half, MID[0], [(other[1],)], mods, gains, weights, keys, values, late=True
    )
    one = attend(0, LAST[:1], counts, query, keys, values, proj)
    two = attend(LAST[0], LAST[1:], counts, query, keys, values, proj)
    got = [exchange(block) for block in (*one, *two)]
    rest = late_query(hidden, gains, weights, two[0])
    base = attend(0, LAST, counts, (query_other, rest), keys, values, proj, other, mods)
    done = [move(combine(b, g, mods)) for b, g in zip(base, got)]
    return jnp.concatenate(done, axis=0)[None]


def solution(mesh):
    in_specs = (
        P("section", "cfg", None),
        P(),
        P(),
        P(),
        P("section", None, None, None),
        P("section", None, None),
        P("section", None, None, "cfg"),
        P("section", "cfg", None),
        P("section", None, "cfg"),
        P("section", None, "cfg"),
    )
    out_specs = P("section", "cfg", None)
    return jax.shard_map(
        on_device, mesh=mesh, in_specs=in_specs, out_specs=out_specs, check_vma=False
    )
```

```python
import jax
import jax.numpy as jnp
from jax import lax
from jax.experimental import pallas as pl
from jax.experimental.pallas import tpu as pltpu
from jax.sharding import PartitionSpec as P

HD = 128
PATCH_TOK = 384
NPATCH = 4
TEXT = 256
SECTIONS = 64
BF16 = jnp.bfloat16
F32 = jnp.float32
VMEM = pl.BlockSpec(memory_space=pltpu.VMEM)
SMEM = pl.BlockSpec(memory_space=pltpu.SMEM)
HBM = pl.BlockSpec(memory_space=pltpu.HBM)
LOOSE = pl.BlockSpec(memory_space=pl.ANY)
MIB = 1024 * 1024
QUERY_SCALE = HD ** (-0.5) * 1.4426950408889634
BLOCK = 1536
MID = (96, 96)
LAST = (80, 64, 48)


def held(array):
    return pltpu.with_memory_space_constraint(array, pltpu.VMEM)


def far(array):
    return pltpu.with_memory_space_constraint(array, pltpu.HBM)


def in_vmem(shape, dtype):
    return pltpu.VMEM(shape, dtype)


def loose(shape, dtype):
    return jax.ShapeDtypeStruct(shape, dtype)


def modulated(rows, mods):
    wide = rows.astype(F32)
    mean = jnp.mean(wide, axis=-1, keepdims=True)
    centred = wide - mean
    spread = jnp.mean(centred * centred, axis=-1, keepdims=True)
    normed = centred * lax.rsqrt(spread + 1e-06)
    return (normed * (1.0 + mods[1:2]) + mods[0:1]).astype(BF16)


def head_norm(proj, gain):
    parts = []
    for head in range(proj.shape[1] // HD):
        x = proj[:, head * HD : (head + 1) * HD]
        scale = lax.rsqrt(jnp.mean(x * x, axis=-1, keepdims=True) + 1e-06)
        parts.append((x * scale * gain).astype(BF16))
    return jnp.concatenate(parts, axis=1)


def project(hidden, weights):
    return jnp.dot(hidden, weights, preferred_element_type=F32)


def limit(mib):
    return pltpu.CompilerParams(vmem_limit_bytes=mib * MIB)


def cost(flops):
    return pl.CostEstimate(flops=int(flops), bytes_accessed=1000000, transcendentals=0)


def first_row(tick, side, patch_index, half):
    section, group = lax.axis_index("section"), lax.axis_index("cfg")
    source = lax.rem(section + SECTIONS - tick, SECTIONS)
    swapped = 0 if tick == 0 else 1 - lax.rem(section, 2)
    which = lax.rem(group + swapped + side, 2)
    return pl.multiple_of(TEXT + patch_index[source] * PATCH_TOK + which * half, 32)


def projections(hidden, gains, weights, waits, put_key, put_value, query):
    waits[0]()
    put_key(head_norm(project(hidden, weights[1]), gains[1:2]))
    waits[1]()
    put_value(project(hidden, weights[2]).astype(BF16))
    waits[2]()
    query[...] = head_norm(project(hidden, weights[0]), gains[0:1] * QUERY_SCALE)


def selected(modulation, step):
    at = lax.broadcasted_iota(jnp.int32, (modulation.shape[1], 1), 0) == step
    rows = [
        jnp.sum(jnp.where(at, modulation[i].astype(F32), 0.0), axis=0, keepdims=True)
        for i in range(modulation.shape[0])
    ]
    return jnp.concatenate(rows, axis=0)


def open_kernel(
    patch_far, step_far, rows_far, modulation_far, gains_far, w_qkv_far, w_out_far, keys_far, values_far,
    query, rows, upper, lower, mods_now, mods_next, gains, w_qkv, w_out, keys, values,
    modulation, patch_index, step_index, sems, more,
):
    pairs = [
        (patch_far, patch_index),
        (step_far, step_index),
        (gains_far, gains),
        (modulation_far, modulation),
        (rows_far, rows),
        (keys_far, keys),
        (values_far, values),
        (w_out_far, w_out),
    ]
    others = [pltpu.make_async_copy(a, b, more.at[i]) for i, (a, b) in enumerate(pairs)]
    for copy in others[:5]:
        copy.start()
    copies = [pltpu.make_async_copy(w_qkv_far.at[i], w_qkv.at[i], sems.at[i]) for i in (1, 2, 0)]
    for copy in copies + others[5:]:
        copy.start()
    section = lax.axis_index("section")
    for copy in others[:4]:
        copy.wait()
    mods = selected(modulation, step_index[section])
    mods_now[...] = mods
    mods_next[...] = selected(modulation, step_index[lax.rem(section + SECTIONS - 1, SECTIONS)])
    others[4].wait()
    upper[...] = rows[: upper.shape[0], :]
    lower[...] = rows[upper.shape[0] :, :]
    hidden = modulated(rows[...], mods)
    here = pl.ds(first_row(0, 0, patch_index, rows.shape[0]), rows.shape[0])

    def put_key(fresh):
        others[5].wait()
        keys[here, :] = fresh

    def put_value(fresh):
        others[6].wait()
        values[here, :] = fresh

    projections(hidden, gains[...], w_qkv, [c.wait for c in copies], put_key, put_value, query)
    others[7].wait()


def opening(patch_index, step_index, rows, modulation, gains, w_qkv, w_out, keys, values):
    model = rows.shape[1]
    return pl.pallas_call(
        open_kernel,
        in_specs=[HBM] * 9,
        out_specs=[VMEM] * 11,
        out_shape=[
            in_vmem((rows.shape[0], keys.shape[1]), BF16),
            in_vmem(rows.shape, BF16),
            loose((MID[0], model), BF16),
            loose((MID[1], model), BF16),
            loose((3, model), F32),
            loose((3, model), F32),
            loose(gains.shape, F32),
            in_vmem(w_qkv.shape, BF16),
            in_vmem(w_out.shape, BF16),
            in_vmem(keys.shape, BF16),
            in_vmem(values.shape, BF16),
        ],
        scratch_shapes=[
            pltpu.VMEM(modulation.shape, BF16),
            pltpu.SMEM(patch_index.shape, jnp.int32),
            pltpu.SMEM(step_index.shape, jnp.int32),
            pltpu.SemaphoreType.DMA((3,)),
            pltpu.SemaphoreType.DMA((8,)),
        ],
        compiler_params=limit(16),
        cost_estimate=cost(2 * w_qkv.size * 256),
        name="opening",
    )(*map(far, (patch_index, step_index, rows, modulation, gains, w_qkv, w_out, keys, values)))


def qkv(tick, side, patch_index, half, offset, pairs, mods, gains, w_qkv, keys, values, late=False):
    count, width = sum(p[0].shape[0] for p in pairs), keys.shape[1]
    n = sum(map(len, pairs))

    def kernel(patch_index, *refs):
        parts, (mods, gains, w_qkv, _, _) = refs[:n], refs[n : n + 5]
        query, keys, values = refs[n + 5 :]
        rows, place = [], 0
        for p in pairs:
            one, *two = [ref[...] for ref in parts[place : place + len(p)]]
            rows.append(one + jnp.concatenate(two, axis=0) if two else one)
            place += len(p)
        hidden = modulated(rows[0] if len(pairs) == 1 else jnp.concatenate(rows, axis=0), mods[...])
        here = pl.ds(pl.multiple_of(first_row(tick, side, patch_index, half) + offset, 32), count)
        if late:
            query[...] = hidden
        keys[here, :] = head_norm(project(hidden, w_qkv[1]), gains[1:2])
        values[here, :] = project(hidden, w_qkv[2]).astype(BF16)
        if not late:
            query[...] = head_norm(project(hidden, w_qkv[0]), gains[0:1] * QUERY_SCALE)

    return pl.pallas_call(
        kernel,
        in_specs=[SMEM] + [VMEM] * (n + 5),
        out_specs=[VMEM] * 3,
        out_shape=[
            in_vmem((count, pairs[0][0].shape[1] if late else width), BF16),
            in_vmem(keys.shape, BF16),
            in_vmem(values.shape, BF16),
        ],
        input_output_aliases={n + 4: 1, n + 5: 2},
        compiler_params=limit(16),
        cost_estimate=cost(2 * w_qkv.size * 256),
        name="qkv",
    )(patch_index, *(a for p in pairs for a in p), mods, gains, held(w_qkv), held(keys), held(values))


def late_query_kernel(hidden, gains, w_qkv, after, query):
    del after
    query[...] = head_norm(project(hidden[...], w_qkv[0]), gains[0:1] * QUERY_SCALE)


def late_query(hidden, gains, w_qkv, after):
    return pl.pallas_call(
        late_query_kernel,
        in_specs=[VMEM] * 3 + [LOOSE],
        out_specs=VMEM,
        out_shape=in_vmem((hidden.shape[0], w_qkv.shape[2]), BF16),
        compiler_params=limit(16),
        cost_estimate=cost(2 * w_qkv.size * 256 / 3),
        name="late_query",
    )(held(hidden), gains, held(w_qkv), after)


def attended(query, keys, values, counts):
    total = keys.shape[0]
    place = lax.broadcasted_iota(jnp.int32, (1, total), 1)
    valid = place < TEXT
    for patch in range(NPATCH):
        begin = TEXT + patch * PATCH_TOK
        valid |= (place >= begin) & (place < begin + counts[patch])
    bias = jnp.where(valid, 0.0, -1e30)
    ones = jnp.ones((total, HD), BF16)
    outs = []
    for head in range(keys.shape[1] // HD):
        cols = slice(head * HD, (head + 1) * HD)
        scores = lax.dot_general(
            query[:, cols], keys[:, cols], (((1,), (1,)), ((), ())), preferred_element_type=F32
        )
        scores = scores + bias
        expo = jnp.exp2(scores - jnp.max(scores, axis=-1, keepdims=True)).astype(BF16)
        out = project(expo, jnp.concatenate([values[:, cols], ones], axis=1))
        outs.append((out[:, :HD] / out[:, HD:]).astype(BF16))
    return jnp.concatenate(outs, axis=1)


def attend(begin, sizes, counts, query, keys, values, w_out, pieces=(), mods=None):
    count, model = sum(sizes), w_out.shape[1]
    keep = len(pieces) > 0
    whole = not keep and begin == 0
    queries = query if isinstance(query, tuple) else (query,)
    n, k = len(pieces), len(queries)

    def kernel(counts, *refs):
        query, (keys, values, w_out), refs = refs[:k], refs[k : k + 3], refs[k + 3 :]
        out, outs = refs[-1], refs[-1 - len(sizes) : -1]
        if k == 1:
            rows = query[0][begin : begin + count, :]
        else:
            rows = jnp.concatenate([q[...] for q in query], axis=0)
        out[...] = attended(rows, keys, values, counts)

        def columns(i, carry):
            cols = pl.ds(0, model) if whole else pl.ds(pl.multiple_of(i * BLOCK, BLOCK), BLOCK)
            mixed = project(out[...], w_out[:, cols])
            if keep:
                rows = jnp.concatenate([p[:, cols] for p in refs[:n]], axis=0)
                mixed = rows.astype(F32) + refs[n][2:3, cols] * mixed
            place = 0
            for ref, size in zip(outs, sizes):
                ref[:, cols] = mixed[place : place + size].astype(ref.dtype)
                place += size
            return carry

        if whole:
            columns(0, 0)
        else:
            lax.fori_loop(0, model // BLOCK, columns, 0)

    extra = (*pieces, mods) if keep else ()
    return pl.pallas_call(
        kernel,
        in_specs=[SMEM] + [VMEM] * (3 + k + len(extra)),
        out_specs=[VMEM] * len(sizes),
        out_shape=[in_vmem((size, model), F32 if keep else BF16) for size in sizes],
        scratch_shapes=[pltpu.VMEM((count, keys.shape[1]), BF16)],
        compiler_params=limit(16),
        cost_estimate=cost(2 * 256 * keys.shape[1] * (2 * keys.shape[0] + model)),
        name="attend",
    )(counts, *map(held, queries), held(keys), held(values), held(w_out), *extra)


def combine_kernel(base, received, mods, out):
    out[...] = (base[...] + mods[2:3] * received[...].astype(F32)).astype(BF16)


def combine(base, received, mods):
    return pl.pallas_call(
        combine_kernel,
        in_specs=[VMEM] * 3,
        out_specs=VMEM,
        out_shape=in_vmem(received.shape, BF16),
        compiler_params=limit(6),
        name="combine",
    )(held(base), held(received), mods)


def on_device(
    patches, patch_index, step_index, counts, modulation, qk_gain, w_qkv, w_out, cache_k, cache_v
):
    both = ("section", "cfg")
    swap = [(2 * s + c, 2 * s + 1 - c) for s in range(SECTIONS) for c in range(2)]
    shift = [
        (2 * s + c, 2 * ((s + 1) % SECTIONS) + (c if s % 2 == 0 else 1 - c))
        for s in range(SECTIONS)
        for c in range(2)
    ]

    def exchange(block):
        return lax.ppermute(block, both, swap)

    def move(block):
        return lax.ppermute(block, both, shift)

    own = patches[0]
    early = lax.ppermute(own, both, [p for p in swap if p[0] // 2 % 2 == 0])
    query, copied, upper, lower, mods, mods_next, gains, weights, proj, keys, values = opening(
        patch_index, step_index, own, jnp.transpose(modulation[0], (1, 0, 2)), qk_gain[0], w_qkv[0],
        w_out[0], cache_k[0], cache_v[0],
    )
    late = [lax.ppermute(piece, both, [p for p in swap if p[0] // 2 % 2 == 1]) for piece in (upper, lower)]
    query_other, keys, values = qkv(
        0, 1, patch_index, own.shape[0], 0, [(early, *late)], mods, gains, weights, keys, values
    )
    begin = 0
    got = []
    for size in MID:
        got.append(exchange(attend(begin, (size,), counts, query_other, keys, values, proj)[0]))
        begin += size
    base = attend(0, MID, counts, query, keys, values, proj, (copied,), mods)
    own = [move(combine(b, g, mods)) for b, g in zip(base, got)]

    mods = mods_next
    other = [exchange(block) for block in own]
    half = patches.shape[1]
    query, keys, values = qkv(1, 0, patch_index, half, 0, [(p,) for p in own], mods, gains, weights, keys, values)
    query_other, keys, values = qkv(
        1, 1, patch_index, half, 0, [(other[0],)], mods, gains, weights, keys, values
    )
    hidden, keys, values = qkv(
        1, 1, patch_index, half, MID[0], [(other[1],)], mods, gains, weights, keys, values, late=True
    )
    one = attend(0, LAST[:1], counts, query, keys, values, proj)
    two = attend(LAST[0], LAST[1:], counts, query, keys, values, proj)
    got = [exchange(block) for block in (*one, *two)]
    rest = late_query(hidden, gains, weights, two[0])
    base = attend(0, LAST, counts, (query_other, rest), keys, values, proj, other, mods)
    done = [move(combine(b, g, mods)) for b, g in zip(base, got)]
    return jnp.concatenate(done, axis=0)[None]


def solution(mesh):
    in_specs = (
        P("section", "cfg", None),
        P(),
        P(),
        P(),
        P("section", None, None, None),
        P("section", None, None),
        P("section", None, None, "cfg"),
        P("section", "cfg", None),
        P("section", None, "cfg"),
        P("section", None, "cfg"),
    )
    out_specs = P("section", "cfg", None)
    return jax.shard_map(
        on_device, mesh=mesh, in_specs=in_specs, out_specs=out_specs, check_vma=False
    )
```
